1024 devices in a mesh: expert: 64 (over x, z_lo), fsdp: 16 (over y, z_hi, core).
Axes of the slice: x: 4, y: 4, z: 32 (z_hi: 2, z_lo: 16; z = z_hi * 16 + z_lo), core: 2. Of those that a mesh axis runs over, the one named last changes fastest.
Arguments:
- tokens: bfloat16 [1536, 5120], P('expert', 'fsdp'), may hold values from -6 to 6
- route: int32 [1536, 1], P('expert'), may hold values from 0 to 3; in each aligned block of 24 rows (0 to 23, 24 to 47, ...) at most 8 rows name the same one
- score: bfloat16 [1536], P('expert'), may hold values from 0.099609375 to 1
- grad_out: bfloat16 [1536, 5120], P('expert', 'fsdp'), may hold values from -1.1953125 to 1.1953125
- w_gate: bfloat16 [5120, 32768], P('fsdp', 'expert'), may hold values from -0.078125 to 0.078125
- w_up: bfloat16 [5120, 32768], P('fsdp', 'expert'), may hold values from -0.078125 to 0.078125
- w_down: bfloat16 [32768, 5120], P('expert', 'fsdp'), may hold values from -0.0625 to 0.0625
Outputs:
- grad_tokens: bfloat16 [1536, 5120], P('expert', 'fsdp')
- grad_score: float32 [1536], P('expert')
- grad_gate: bfloat16 [5120, 32768], P('fsdp', 'expert')
- grad_up: bfloat16 [5120, 32768], P('fsdp', 'expert')
- grad_down: bfloat16 [32768, 5120], P('expert', 'fsdp')
The draws below stay inside these ranges and needn't reach their ends.
Inputs may be any that keep to these rules, and one draw needn't show every extreme that they name: `route`: among the 24 tokens of each block, no expert is named more than 8 times; some block names some expert exactly 8 times.
All inputs are finite; a program needn't handle non-finite values.
Results may differ from the reference program's by a relative error of at most 0.0095.
Values may be sent and summed in bfloat16 or wider, within the bound.
A program may use at most 32 MiB of HBM per device.

```python
import math
import jax
import jax.numpy as jnp
import numpy as np
from jax import lax

D = 5120
HIDDEN_SIZE = 8192
EXPERTS = 4
TOK_DEV = 24
MOST = 8
TOKENS = 1536
N_EXPERT = 64


def block_levels(key, shape, cuts, least, high):
    loudness = 1.0
    for position, shards_of in cuts:
        heights = jax.random.uniform(jax.random.fold_in(jax.random.fold_in(key, 6), position), (shards_of,), jnp.float32, least / len(cuts), high / len(cuts))
        loudness = loudness * jnp.repeat(jnp.exp(heights), shape[position] // shards_of).reshape((-1,) + (1,) * (len(shape) - 1 - position))
    return loudness


def assign_block(rng, own, number, rows, count, top, bound, lean):
    sequence = jax.random.permutation(rng, count)
    packed, usual = portions_of(count, rows * top, bound, lean, True), portions_of(count, rows * top, bound, lean, False)
    places = jnp.arange(count)

    def named(sizes, turn):
        used = int((sizes > 0).sum())
        fixed = max(1, used // 4)
        passed = fixed + (places - fixed + turn * (used - fixed)) % max(1, count - fixed)
        return jnp.zeros((count,), jnp.int32).at[sequence[jnp.where(places < fixed, places, passed)]].set(jnp.asarray(sizes, jnp.int32))

    sizes = jnp.where(number % 4 == 0, named(packed, number // 4), named(usual, number - number // 4 - 1))
    mixed = jax.random.permutation(jax.random.fold_in(own, 3), count)
    donor, receiver = mixed[0:count // 2 * 2:2], mixed[1:count // 2 * 2:2]
    room = jnp.minimum(sizes[donor] - 1, bound - sizes[receiver]) // 2
    room = jnp.where((donor == sequence[0]) | (receiver == sequence[0]) | (sizes[receiver] == 0), 0, jnp.maximum(room, 0))
    passed = jax.random.randint(jax.random.fold_in(own, 4), (count // 2,), 0, 1 << 20) % (room + 1)
    sizes = sizes.at[donor].add(-passed).at[receiver].add(passed)
    members = jnp.searchsorted(jnp.cumsum(sizes), jnp.arange(rows * top), side="right").astype(jnp.int32)
    listing = members.reshape(top, rows).T
    listing = listing[jax.random.permutation(jax.random.fold_in(own, 1), rows)]
    turn = jax.random.randint(jax.random.fold_in(own, 2), (rows, 1), 0, top)
    return jnp.take_along_axis(listing, (jnp.arange(top)[None, :] + turn) % top, axis=1)


def portions_of(number_of, total, limit, skew, full):
    portions = [(1 << 20) // math.isqrt(rank ** skew) + 1 for rank in range(1, number_of + 1)]
    largest = limit if full else min(limit, max(-(-total // number_of), total * portions[0] // sum(portions)))
    least = 1 if total - largest >= number_of - 1 else 0
    counts, rest = [largest] + [least] * (number_of - 1), total - largest - least * (number_of - 1)
    while rest > 0:
        candidates = [i for i in range(1, number_of) if counts[i] < largest] or [i for i in range(1, number_of) if counts[i] < limit]
        whole, left = sum([portions[i] for i in candidates]), rest
        for i in candidates:
            extra = min(limit - counts[i], max(1, left * portions[i] // whole), rest)
            counts[i] = counts[i] + extra
            rest = rest - extra
    return np.array(counts)


def bell_draw(own_key, shape, width, most, pieces=(), held_as=jnp.bfloat16):
    loudness = block_levels(own_key, shape, pieces, -0.22, 0.18) if pieces else 1.0
    entries = jax.random.normal(own_key, shape, jnp.float32) * width * loudness
    return jnp.minimum(jnp.maximum(entries, -most), most).astype(held_as)


def setup_inputs(seed: int = 0) -> dict:
    arg_keys = jax.random.split(jax.random.key(seed), 8)
    tokens = bell_draw(arg_keys[0], (TOKENS, D), 1.0, 6.0, ((0, 64), (1, 16)))
    route_keys = jax.random.split(jax.random.fold_in(arg_keys[1], 1), TOKENS // TOK_DEV)
    route_turns = jax.random.permutation(jax.random.fold_in(arg_keys[1], 3), TOKENS // TOK_DEV)
    route = jax.vmap(lambda own, number: assign_block(jax.random.fold_in(arg_keys[1], 2), own, number, TOK_DEV, EXPERTS, 1, MOST, 2))(route_keys, route_turns).reshape((TOKENS, 1))
    score = jnp.clip(0.099609375 + 0.9003906 * jax.random.uniform(arg_keys[2], (TOKENS,), jnp.float32) ** block_levels(arg_keys[2], (TOKENS,), ((0, 64),), -0.2, 0.2), 0.099609375, 1.0).astype(jnp.bfloat16)
    grad_out = bell_draw(arg_keys[3], (TOKENS, D), 0.2, 1.1953125, ((0, 64), (1, 16)))
    w_gate = bell_draw(arg_keys[4], (D, EXPERTS * HIDDEN_SIZE), D ** -0.5, 0.078125, ((0, 16), (1, 64)))
    w_up = bell_draw(arg_keys[5], (D, EXPERTS * HIDDEN_SIZE), D ** -0.5, 0.078125, ((0, 16), (1, 64)))
    w_down = bell_draw(arg_keys[6], (EXPERTS * HIDDEN_SIZE, D), HIDDEN_SIZE ** -0.5, 0.0625, ((0, 64), (1, 16)))
    return {"tokens": tokens, "route": route, "score": score, "grad_out": grad_out, "w_gate": w_gate, "w_up": w_up, "w_down": w_down}


def activate(gate_vals, up_vals, back_vals, slot_scale):
    sigmoid_gate = jax.nn.sigmoid(gate_vals)
    silu_gate = gate_vals * sigmoid_gate
    hidden_vals = silu_gate * up_vals
    scaled_hidden = (slot_scale[:, None] * hidden_vals).astype(jnp.bfloat16)
    proj_grad = slot_scale[:, None] * back_vals
    gate_grad = (proj_grad * up_vals * sigmoid_gate * (1.0 + gate_vals * (1.0 - sigmoid_gate))).astype(jnp.bfloat16)
    up_grad = (proj_grad * silu_gate).astype(jnp.bfloat16)
    return scaled_hidden, gate_grad, up_grad, hidden_vals * back_vals


def reference(tokens, route, score, grad_out, w_gate, w_up, w_down):
    shard_count = N_EXPERT // EXPERTS
    slot_rows = N_EXPERT * MOST
    blocks = route.reshape(N_EXPERT, TOK_DEV)
    expert_ids = jnp.arange(EXPERTS, dtype=jnp.int32)
    onehot = (blocks[:, :, None] == expert_ids[None, None, :]).astype(jnp.int32)
    ranks_local = jnp.cumsum(onehot, axis=1) - 1
    slot_ids = jnp.arange(MOST, dtype=jnp.int32)
    placement = ((onehot[:, :, :, None] == 1) & (ranks_local[:, :, :, None] == slot_ids[None, None, None, :])).astype(jnp.float32)
    token_blocks = tokens.reshape(N_EXPERT, TOK_DEV, D).astype(jnp.float32)
    grad_blocks = grad_out.reshape(N_EXPERT, TOK_DEV, D).astype(jnp.float32)
    score_blocks = score.reshape(N_EXPERT, TOK_DEV).astype(jnp.float32)
    slot_tokens = jnp.einsum('btem,btd->ebmd', placement, token_blocks).astype(jnp.bfloat16).reshape(EXPERTS, slot_rows, D)
    slot_grads = jnp.einsum('btem,btd->ebmd', placement, grad_blocks).astype(jnp.bfloat16).reshape(EXPERTS, slot_rows, D)
    slot_scores = jnp.einsum('btem,bt->ebm', placement, score_blocks).reshape(EXPERTS, slot_rows)

    def one_expert(index):
        first_col = (index * HIDDEN_SIZE).astype(jnp.int32)
        gate_weight = lax.dynamic_slice_in_dim(w_gate, first_col, HIDDEN_SIZE, 1)
        up_weight = lax.dynamic_slice_in_dim(w_up, first_col, HIDDEN_SIZE, 1)
        down_weight = lax.dynamic_slice_in_dim(w_down, first_col, HIDDEN_SIZE, 0)
        rows_in = slot_tokens[index]
        grads_in = slot_grads[index]
        gate_vals = jnp.dot(rows_in, gate_weight, preferred_element_type=jnp.float32)
        up_vals = jnp.dot(rows_in, up_weight, preferred_element_type=jnp.float32)
        back_vals = lax.dot_general(grads_in, down_weight, (((1,), (1,)), ((), ())), preferred_element_type=jnp.float32)
        scaled_hidden, gate_grad, up_grad, products = activate(gate_vals, up_vals, back_vals, slot_scores[index])
        score_piece = products.reshape(slot_rows, shard_count, HIDDEN_SIZE // shard_count).sum(-1).astype(jnp.bfloat16)
        score_piece = lax.optimization_barrier(score_piece)
        score_total = score_piece.astype(jnp.float32).sum(-1)
        grad_gate_e = lax.dot_general(rows_in, gate_grad, (((0,), (0,)), ((), ())), preferred_element_type=jnp.float32).astype(jnp.bfloat16)
        grad_up_e = lax.dot_general(rows_in, up_grad, (((0,), (0,)), ((), ())), preferred_element_type=jnp.float32).astype(jnp.bfloat16)
        grad_down_e = lax.dot_general(scaled_hidden, grads_in, (((0,), (0,)), ((), ())), preferred_element_type=jnp.float32).astype(jnp.bfloat16)
        group_cols = HIDDEN_SIZE // shard_count
        token_piece = jnp.einsum('rsh,dsh->rsd', gate_grad.astype(jnp.float32).reshape(slot_rows, shard_count, group_cols), gate_weight.astype(jnp.float32).reshape(D, shard_count, group_cols))
        token_piece = token_piece + jnp.einsum('rsh,dsh->rsd', up_grad.astype(jnp.float32).reshape(slot_rows, shard_count, group_cols), up_weight.astype(jnp.float32).reshape(D, shard_count, group_cols))
        token_piece = lax.optimization_barrier(token_piece.astype(jnp.bfloat16))
        token_total = token_piece.astype(jnp.float32).sum(1)
        return token_total, score_total, grad_gate_e, grad_up_e, grad_down_e

    token_total, score_total, grad_gate_all, grad_up_all, grad_down_all = lax.map(one_expert, jnp.arange(EXPERTS, dtype=jnp.int32))
    token_total = token_total.reshape(EXPERTS, N_EXPERT, MOST, D)
    score_total = score_total.reshape(EXPERTS, N_EXPERT, MOST)
    grad_tokens = jnp.einsum('btem,ebmd->btd', placement, token_total).astype(jnp.bfloat16).reshape(TOKENS, D)
    grad_score = jnp.einsum('btem,ebm->bt', placement, score_total).reshape(TOKENS)
    grad_gate = jnp.transpose(grad_gate_all, (1, 0, 2)).reshape(D, EXPERTS * HIDDEN_SIZE)
    grad_up = jnp.transpose(grad_up_all, (1, 0, 2)).reshape(D, EXPERTS * HIDDEN_SIZE)
    grad_down = grad_down_all.reshape(EXPERTS * HIDDEN_SIZE, D)
    return grad_tokens, grad_score, grad_gate, grad_up, grad_down
```

```python
import jax
import jax.numpy as jnp
from jax import lax
from jax.experimental import pallas as pl
from jax.experimental.pallas import tpu as pltpu
from jax.sharding import PartitionSpec as P

MESH = pl.DeviceIdType.MESH
MOST = 8
FOUR = 4
CHUNK = 128
QUARTER = 16
ORDER = (
    *("p1", "l0", "p2", "t1", "l1", "t2", "p3", "l2", "t3"),
    *("a2", "l3", "c2", "a3", "c3", "a1", "c1", "a0", "c0"),
    *("d2", "d3", "f2", "d1", "f3", "g2", "d0", "f1", "g3", "f0", "g1", "g0", "w0"),
)


def flip(v, m):
    hi, lo = v // 2, v % 2
    if m & 2:
        hi = 1 - hi
    if m & 1:
        lo = 1 - lo
    return hi * 2 + lo


def kernel(
    h_tokens, h_grads, route_col, route_row, score_row, h_gate, h_up, h_down,
    out_tokens, out_score, out_gate, out_up, out_down,
    tokens, grads, wpad, wd, xs, xr, disp, own, half, y_s, y_r, z_s, z_r, acts,
    tp, c1_r, c2_s, c2_r, fin, back_r,
    s_in, s_x, r_x, s_st, r_st, s_lo, r_lo, s_y, r_y, s_z, r_z,
    s_ya, r_ya, s_c1, r_c1, s_c2, r_c2, s_b, r_b, known,
):
    f32, bf16 = jnp.float32, jnp.bfloat16
    toks, width = tokens.shape
    hid = wd.shape[1]
    wide = tp.shape[-1]
    lead = width // 128 * 128
    off = width - lead
    e = lax.axis_index("expert")
    f = lax.axis_index("fsdp")
    x, q, p = e // 16, (e // 4) % 4, e % 4
    y, zh, c = f // 4, (f // 2) % 2, f % 2
    inner = (q == 1) | (q == 2)
    middle = (p == 1) | (p == 2)
    group = [q, flip(q, 1), 2 - q // 2, 3 - 3 * (q // 2)]

    def at_x(m):
        return (flip(x, m) * 16 + q * 4 + p, f)

    def at_g(g):
        return (x * 16 + g * 4 + p, f)

    def at_p(m):
        return (x * 16 + q * 4 + flip(p, m), f)

    def at_peer(d, m):
        return (e, flip(y, m) * 4 + zh * 2 + (1 - c if d else c))

    def along_z(step):
        z = (zh * 16 + q * 4 + p + step + 32) % 32
        return (x * 16 + z % 16, y * 4 + (z // 16) * 2 + c)

    at_z = along_z(16)
    peers = [(0, 2), (1, 2), (0, 1), (1, 1), (0, 3), (1, 3), (1, 0)]

    def remote(src, dst, send, recv, to):
        return pltpu.make_async_remote_copy(
            src_ref=src, dst_ref=dst, send_sem=send, recv_sem=recv, device_id=to, device_id_type=MESH
        )

    partners = [at(m) for at in (at_x, at_p) for m in (1, 2, 3)]
    partners += [along_z(4), along_z(-4)] + [at_peer(d, m) for d, m in peers]
    barrier = pltpu.get_barrier_semaphore()
    for to in partners:
        pl.semaphore_signal(barrier, inc=1, device_id=to, device_id_type=MESH)

    loads = [
        pltpu.make_async_copy(src, dst, s_in.at[i])
        for i, (src, dst) in enumerate(
            (
                (h_tokens, tokens),
                (h_grads, grads),
                (h_gate, wpad.at[0, 0:width]),
                (h_up, wpad.at[1, 0:width]),
                (h_down, wd.at[off : off + width]),
            )
        )
    ]
    for copy in loads:
        copy.start()

    col = route_col[...]
    row = route_row[...]
    t_row = lax.broadcasted_iota(jnp.int32, (toks, toks), 0)
    t_col = lax.broadcasted_iota(jnp.int32, (toks, toks), 1)
    same = col == row
    rank_col = jnp.sum(jnp.where(same & (t_col < t_row), 1.0, 0.0), axis=1, keepdims=True)
    rank_row = jnp.sum(jnp.where(same & (t_row < t_col), 1.0, 0.0), axis=0, keepdims=True)

    def expert_of(m):
        xh, xl = x // 2, x % 2
        mh, ml = m // 2, m % 2
        return jnp.where(mh == 1, 1 - xh, xh) * 2 + jnp.where(ml == 1, 1 - xl, xl)

    slot_l = lax.broadcasted_iota(jnp.int32, (toks, 32), 1)
    slot_s = lax.broadcasted_iota(jnp.int32, (32, toks), 0)
    place = jnp.where(
        (col == expert_of(slot_l // MOST)) & (rank_col == (slot_l % MOST).astype(f32)), 1.0, 0.0
    )
    place_t = jnp.where(
        (row == expert_of(slot_s // MOST)) & (rank_row == (slot_s % MOST).astype(f32)), 1.0, 0.0
    )
    packed_s = jnp.sum(place_t * score_row[...], axis=1, keepdims=True)
    blank = jnp.zeros((32, wide - width), f32)
    loads[0].wait()
    loads[1].wait()
    packed_t = jnp.dot(place_t.astype(bf16), tokens[...], preferred_element_type=f32)
    packed_g = jnp.dot(place_t.astype(bf16), grads[...], preferred_element_type=f32)
    packed_t = jnp.concatenate([packed_t, blank], axis=1)
    packed_g = jnp.concatenate([packed_g * packed_s, blank], axis=1)
    for m in range(FOUR):
        xs[m] = jnp.concatenate(
            [packed_t[m * 8 : m * 8 + 8], packed_g[m * 8 : m * 8 + 8]], axis=0
        ).astype(bf16)

    pl.semaphore_wait(barrier, len(partners))

    sent = []

    def go(copy):
        copy.start()
        sent.append(copy)
        return copy

    def go_if(cond, copy):
        pl.when(cond)(copy.start)
        sent.append((cond, copy))

    def tell(hop):
        if hop:
            pl.semaphore_wait(known.at[hop - 1], 1)
        if hop < 3:
            pl.semaphore_signal(
                known.at[hop], inc=1, device_id=along_z(4), device_id_type=MESH
            )

    inx = [go(remote(xs.at[m], xr.at[m], s_x.at[m], r_x.at[m], at_x(m))) for m in (1, 2, 3)]
    tell(0)
    wpad[0, width:wide] = jnp.zeros((wide - width, hid), bf16)
    wpad[1, width:wide] = jnp.zeros((wide - width, hid), bf16)
    wd[0:off] = jnp.zeros((off, hid), bf16)
    for copy in inx:
        copy.wait_recv()
    got = [xs[0].astype(f32)] + [xr[m].astype(f32) for m in (1, 2, 3)]
    rows_t = jnp.concatenate([g[0:8, 0:width] for g in got], axis=0)
    rows_g = jnp.concatenate([g[8:16, 0:width] for g in got], axis=0)
    disp[q, p] = jnp.concatenate([rows_t, rows_g], axis=1).astype(bf16)

    def stride(i, to, n):
        unit = disp.at[group[i], p]
        return remote(unit, unit, s_st.at[i, n], r_st.at[group[i]], at_g(to))

    def local(i, whose, to, n):
        unit = disp.at[group[i], whose]
        return remote(unit, unit, s_lo.at[i, n], r_lo.at[group[i], whose], (x * 16 + q * 4 + to, f))

    def local_sends(i):
        go(local(i, p, flip(p, 1), 0))
        go(local(i, p, 2 - p // 2, 1))

    def relay(i):
        def run():
            for n, whose in enumerate((3 - p, flip(p, 2))):
                local(i, whose, flip(p, 1), 2 + n).wait_recv()
                local(i, whose, flip(p, 1), 2 + n).start()

        pl.when(middle)(run)
        for n, whose in enumerate((3 - p, flip(p, 2))):
            sent.append((middle, local(i, whose, flip(p, 1), 2 + n)))

    outer, mate = flip(q, 1), 3 - q
    go(stride(0, outer, 0))
    go_if(inner, stride(0, mate, 1))
    local_sends(0)

    def pass_on(i):
        stride(i, outer, 0).wait_recv()
        go_if(inner, stride(i, mate if i == 1 else outer, 0))
        local_sends(i)

    y_sum = [None] * 4
    z_sum = [None] * 4
    c1 = [None] * 4

    def stage_a(i):
        g = group[i]
        local(i, flip(p, 1), flip(p, 1), 0).wait_recv()

        @pl.when(jnp.logical_not(middle))
        def _():
            for whose in (3 - p, flip(p, 2)):
                local(i, whose, flip(p, 1), 0).wait_recv()

        unit = disp[g].reshape(CHUNK, 2 * width)
        t, u = unit[:, 0:width], unit[:, lead:]
        weights = ((t, wpad[0, 0:width]), (t, wpad[1, 0:width]), (u, wd[...]))
        for n, (rows, weight) in enumerate(weights):
            v = jnp.dot(rows, weight, preferred_element_type=f32)
            v = v.reshape(2, 4, QUARTER, hid)
            own[:, :, :, n * hid : (n + 1) * hid] = v
            y_s[i, :, :, :, n * hid : (n + 1) * hid] = v.astype(bf16)
        y_sum[i] = []
        for d, m in peers:
            block = y_s.at[i, 1 - c if d else c, flip(y, m)]
            k = d * 4 + m
            y_sum[i].append(go(remote(block, y_r.at[i, k], s_y.at[i, k], r_y.at[i, k], at_peer(d, m))))
        half[i] = own[c, y]

    def stage_c(i):
        for copy in y_sum[i]:
            copy.wait_recv()
        v = half[i]
        for d, m in peers:
            v = v + y_r[i, d * 4 + m].astype(f32)
        half[i] = v
        z_s[i] = v.astype(bf16)
        z_sum[i] = go(remote(z_s.at[i], z_r.at[i], s_z.at[i], r_z.at[i], at_z))

    def stage_d(i):
        z_sum[i].wait_recv()
        v = half[i] + z_r[i].astype(f32)
        gate, up, back = v[:, 0:hid], v[:, hid : 2 * hid], v[:, 2 * hid : 3 * hid]
        sig = jax.nn.sigmoid(gate)
        silu = gate * sig
        hidden = silu * up
        acts[i, c, y, :, 0:hid] = (back * up * sig * (1.0 + gate * (1.0 - sig))).astype(bf16)
        acts[i, c, y, :, hid : 2 * hid] = (back * silu).astype(bf16)
        acts[i, c, y, :, 2 * hid : 3 * hid] = hidden.astype(bf16)
        piece = jnp.sum(hidden * back, axis=1, keepdims=True)
        acts[i, c, y, :, 3 * hid : 3 * hid + 128] = jnp.broadcast_to(piece, (QUARTER, 128)).astype(bf16)
        mine = acts.at[i, c, y]
        for d, m in peers:
            k = d * 4 + m
            go(remote(mine, mine, s_ya.at[i, k], r_ya.at[i, k], at_peer(d, m)))

    def stage_f(i):
        for d, m in peers:
            k = d * 4 + m
            theirs = acts.at[i, 1 - c if d else c, flip(y, m)]
            remote(theirs, theirs, s_ya.at[i, k], r_ya.at[i, k], at_peer(d, m)).wait_recv()
        a = acts[i].reshape(CHUNK, acts.shape[-1])
        nt = (((1,), (1,)), ((), ()))
        v = lax.dot_general(a[:, 0:hid], wpad[0], nt, preferred_element_type=f32)
        v = v + lax.dot_general(a[:, hid : 2 * hid], wpad[1], nt, preferred_element_type=f32)
        piece = a[:, 3 * hid : 3 * hid + 1].astype(f32)
        at = lax.broadcasted_iota(jnp.int32, (CHUNK, wide), 1)
        v = jnp.where(at == width, piece, v)
        tp[i] = v.astype(bf16).reshape(4, 32, wide)
        c1[i] = [
            go(remote(tp.at[i, flip(p, m)], c1_r.at[i, m], s_c1.at[i, m], r_c1.at[i, m], at_p(m)))
            for m in (1, 2, 3)
        ]

    def stage_g(i):
        for copy in c1[i]:
            copy.wait_recv()
        v = tp[i, p].astype(f32)
        for m in (1, 2, 3):
            v = v + c1_r[i, m].astype(f32)
        if i == 0:
            fin[...] = v
        else:
            c2_s[i] = v.astype(bf16)
            go(remote(c2_s.at[i], c2_r.at[q], s_c2.at[i], r_c2.at[q], at_g(group[i])))

    def stage_w(_):
        a = acts[...].reshape(4, CHUNK, acts.shape[-1])
        tn = (((0,), (0,)), ((), ()))
        units = jnp.concatenate([disp[g].reshape(CHUNK, 2 * width) for g in group], axis=0)
        ts, gs = units[:, 0:width], units[:, lead:]
        a = a.reshape(4 * CHUNK, acts.shape[-1])
        out_gate[...] = lax.dot_general(ts, a[:, 0:hid], tn, preferred_element_type=f32).astype(bf16)
        out_up[...] = lax.dot_general(ts, a[:, hid : 2 * hid], tn, preferred_element_type=f32).astype(bf16)
        v = lax.dot_general(gs, a[:, 2 * hid : 3 * hid], tn, preferred_element_type=f32)
        out_down[...] = v[off:].astype(bf16)

    stages = {"p": pass_on, "t": tell, "l": relay, "a": stage_a, "c": stage_c, "d": stage_d}
    stages.update({"f": stage_f, "g": stage_g, "w": stage_w})
    loads[2].wait()
    loads[3].wait()
    loads[4].wait()
    for step in ORDER:
        stages[step[0]](int(step[1]))

    for i in (1, 2, 3):
        part = c2_r.at[group[i]]
        remote(part, part, s_c2.at[i], r_c2.at[group[i]], at_g(group[i])).wait_recv()
    v = fin[...]
    for i in (1, 2, 3):
        v = v + c2_r[group[i]].astype(f32)
    fin[...] = v
    back = [
        go(remote(fin.at[pl.ds(m * 8, 8)], back_r.at[m], s_b.at[m], r_b.at[m], at_x(m)))
        for m in (1, 2, 3)
    ]

    for copy in back:
        copy.wait_recv()
    v = jnp.concatenate([fin[0:8]] + [back_r[m] for m in (1, 2, 3)], axis=0)
    total = jnp.sum(place_t * v[:, width : width + 1], axis=0, keepdims=True)
    out_score[...] = total / score_row[...]
    v = jnp.dot(place.astype(bf16), v[:, 0:width].astype(bf16), preferred_element_type=f32)
    out_tokens[...] = v.astype(bf16)

    for item in sent:
        if isinstance(item, tuple):
            pl.when(item[0])(item[1].wait_send)
        else:
            item.wait_send()


def per_device(tokens, route, score, grad_out, w_gate, w_up, w_down):
    toks, width = tokens.shape
    hid = w_gate.shape[1]
    wide = -(-width // 128) * 128
    bf16, f32 = jnp.bfloat16, jnp.float32
    vm = pltpu.VMEM
    dma = pltpu.SemaphoreType.DMA
    scratch = [
        vm((toks, width), bf16),
        vm((toks, width), bf16),
        vm((2, wide, hid), bf16),
        vm((wide, hid), bf16),
        vm((4, 16, wide), bf16),
        vm((4, 16, wide), bf16),
        vm((4, 4, 32, 2 * width), bf16),
        vm((2, 4, QUARTER, 3 * hid), f32),
        vm((4, QUARTER, 3 * hid), f32),
        vm((4, 2, 4, QUARTER, 3 * hid), bf16),
        vm((4, 8, QUARTER, 3 * hid), bf16),
        vm((4, QUARTER, 3 * hid), bf16),
        vm((4, QUARTER, 3 * hid), bf16),
        vm((4, 2, 4, QUARTER, 3 * hid + 128), bf16),
        vm((4, 4, 32, wide), bf16),
        vm((4, 4, 32, wide), bf16),
        vm((4, 32, wide), bf16),
        vm((4, 32, wide), bf16),
        vm((32, wide), f32),
        vm((4, 8, wide), f32),
    ]
    shapes = [(5,)]
    shapes += [(4,), (4,), (4, 2), (4,), (4, 4), (4, 4)]
    shapes += [(4, 8), (4, 8), (4,), (4,)]
    shapes += [(4, 8), (4, 8)]
    shapes += [(4, 4), (4, 4), (4,), (4,), (4,), (4,)]
    scratch += [dma(shape) for shape in shapes]
    scratch.append(pltpu.SemaphoreType.REGULAR((3,)))
    outs = pl.pallas_call(
        kernel,
        out_shape=(
            jax.ShapeDtypeStruct((toks, width), bf16),
            jax.ShapeDtypeStruct((1, toks), f32),
            jax.ShapeDtypeStruct((width, hid), bf16),
            jax.ShapeDtypeStruct((width, hid), bf16),
            jax.ShapeDtypeStruct((width, hid), bf16),
        ),
        in_specs=[pl.BlockSpec(memory_space=pltpu.HBM if i in (0, 1, 5, 6, 7) else vm) for i in range(8)],
        out_specs=(pl.BlockSpec(memory_space=vm),) * 5,
        scratch_shapes=scratch,
        compiler_params=pltpu.CompilerParams(
            collective_id=0, has_side_effects=True, vmem_limit_bytes=60 << 20
        ),
        cost_estimate=pl.CostEstimate(
            flops=16 * 512 * width * hid, bytes_accessed=12 * width * hid, transcendentals=64 * hid
        ),
    )(
        tokens,
        grad_out,
        route,
        route.reshape(1, toks),
        score.astype(f32).reshape(1, toks),
        w_gate,
        w_up,
        w_down.T,
    )
    grad_tokens, grad_score, grad_gate, grad_up, grad_down = outs
    return (grad_tokens, grad_score.reshape(toks), grad_gate, grad_up, grad_down.T)


def solution(mesh):
    return jax.shard_map(
        per_device,
        mesh=mesh,
        in_specs=(
            P("expert", "fsdp"),
            P("expert", None),
            P("expert"),
            P("expert", "fsdp"),
            P("fsdp", "expert"),
            P("fsdp", "expert"),
            P("expert", "fsdp"),
        ),
        out_specs=(
            P("expert", "fsdp"),
            P("expert"),
            P("fsdp", "expert"),
            P("fsdp", "expert"),
            P("expert", "fsdp"),
        ),
        check_vma=False,
    )
```
